32 devices in a mesh: groups: 2 (over x), row: 16 (over z, y, core).
Axes of the slice: x: 2, y: 2, z: 4, core: 2. Of those that a mesh axis runs over, the one named last changes fastest.
Arguments:
- samples: bfloat16 [2, 64, 524288], P(None, 'groups', 'row'), parts along dimension 1, may hold values from -6 to 6
- delay_knots: bfloat16 [2, 64, 16], P(None, 'groups', 'row'), parts along dimension 1, may hold values from -3 to 3
- sample_delays: int32 [64, 16], P('groups'), parts along dimension 0, may hold values from 0 to 4095, as said below
- owner_map: int32 [4096], replicated, may hold values from 0 to 4095, each once
- filter_taps: float32 [4, 4096], replicated, may hold values from -3 to 3
Outputs:
- visibilities: float32 [2, 4, 4096, 1024], P(None, 'groups', 'row'), parts along dimension 1
The draws below stay inside these ranges and needn't reach their ends.
There are 2 independent parts, one for each index of `groups`. The reference program is written for one: setup_inputs(seed, part) draws one part's arguments, and reference() takes and returns one part's arrays. A program takes and returns all parts, laid end to end along the dimension named above; an argument that names none is the same for every part. Nothing has to cross between parts.
Inputs may be any that keep to these rules, and one draw needn't show every extreme that they name: `sample_delays`: whole-sample delays; in every draw some entry is 0 and some entry is 4095. `owner_map`: each channel appears exactly once.
All inputs are finite; a program needn't handle non-finite values.
Results may differ from the reference program's by a relative error of at most 0.0025.
Values may be sent and summed in bfloat16 or wider, within the bound.
A program may use at most 192 MiB of HBM per device.

```python
import math
from functools import partial
import jax
import jax.numpy as jnp
from jax import lax

CHANNELS = 4096
TAPS = 4
STATIONS = 32
FRAMES = 8
DUMP_SEGS = 8
SEGMENTS = 16
TIME = 524288
DUMPS = 2


def draw_sample_delays(key, part):
    key_values = jax.random.fold_in(key, 11)
    key_chosen = jax.random.fold_in(key, 12)
    values = jax.random.randint(key_values, (STATIONS * SEGMENTS,), 0, CHANNELS)
    chosen = jax.random.permutation(key_chosen, STATIONS * SEGMENTS)
    values = values.at[chosen[0]].set(CHANNELS - 1)
    values = values.at[chosen[1]].set(0)
    return values.reshape(STATIONS, SEGMENTS).astype(jnp.int32)


def block_scale(key, extent, pieces, low, top_value):
    loudness, own = 1.0, jax.random.fold_in(key, 6)
    for position, blocks in pieces:
        draws = jnp.exp(jax.random.uniform(jax.random.fold_in(own, position), (blocks,), jnp.float32, low / len(pieces), top_value / len(pieces)))
        loudness = loudness * jnp.repeat(draws, extent[position] // blocks).reshape([-1 if axis == position else 1 for axis in range(len(extent))])
    return loudness


def centred(own_key, shape, width, bound, pieces=(), held_as=jnp.bfloat16):
    factor_of = block_scale(own_key, shape, pieces, -0.22, 0.18) if pieces else 1.0
    array = jax.random.normal(own_key, shape, jnp.float32) * width * factor_of
    return jnp.minimum(jnp.maximum(array, -bound), bound).astype(held_as)


def setup_inputs(seed: int = 0, part: int = 0) -> dict:
    key_of = jax.random.split(jax.random.key(seed), 6)
    own_keys = jax.random.split(jax.random.fold_in(key_of[5], part), 6)
    return {
        "samples": centred(own_keys[0], (2, STATIONS, TIME), 1.0, 6.0, ((2, 16),)),
        "delay_knots": jnp.clip(jax.random.uniform(own_keys[1], (2, STATIONS, SEGMENTS), jnp.float32, -3.0, 3.0) * block_scale(own_keys[1], (2, STATIONS, SEGMENTS), ((2, 16),), -0.4, 0.0), -3.0, 3.0).astype(jnp.bfloat16),
        "sample_delays": draw_sample_delays(jax.random.fold_in(jax.random.fold_in(key_of[5], part), 71), part),
        "owner_map": jax.random.permutation(key_of[3], CHANNELS).astype(jnp.int32),
        "filter_taps": centred(key_of[4], (TAPS, CHANNELS), TAPS ** -0.5, 3.0, (), jnp.float32),
    }


def delayed_rows(window, offset, length):
    return lax.dynamic_slice_in_dim(window, offset, length, axis=1)

def reference(samples, delay_knots, sample_delays, owner_map, filter_taps):
    seg_len = FRAMES * CHANNELS
    history = TAPS - 1
    frames_dump = DUMP_SEGS * FRAMES
    padded = jnp.pad(samples, ((0, 0), (0, 0), (CHANNELS, 0)))
    shifter = jax.vmap(partial(delayed_rows, length=seg_len), in_axes=(1, 0), out_axes=1)
    freq = (jnp.arange(CHANNELS, dtype=jnp.float32) - CHANNELS / 2) / CHANNELS
    weights = (jnp.arange(FRAMES, dtype=jnp.float32) + 1.0) / FRAMES

    def segment_z(segment):
        clamped = jnp.maximum(segment, 0).astype(jnp.int32)
        window = lax.dynamic_slice_in_dim(padded, clamped * seg_len, seg_len + CHANNELS, axis=2)
        offsets = (CHANNELS - sample_delays[:, clamped]).astype(jnp.int32)
        moved = shifter(window, offsets)
        keep = (segment >= 0).astype(moved.dtype)
        return moved * keep

    def one_dump(dump):
        first_seg = dump * DUMP_SEGS
        segs = (first_seg + jnp.arange(DUMP_SEGS, dtype=jnp.int32)).astype(jnp.int32)
        zones = lax.map(segment_z, segs)
        zones = jnp.moveaxis(zones, 0, 2).reshape(2, STATIONS, DUMP_SEGS * seg_len)
        previous = segment_z(first_seg - 1)[:, :, seg_len - history * CHANNELS:]
        extended = jnp.concatenate([previous, zones], axis=2).astype(jnp.float32)
        extended = extended.reshape(2, STATIONS, frames_dump + history, CHANNELS)
        filtered = jnp.zeros((2, STATIONS, frames_dump, CHANNELS), jnp.float32)
        for tap_id in range(TAPS):
            filtered = filtered + filter_taps[tap_id] * extended[:, :, tap_id:tap_id + frames_dump]
        spectrum = jnp.fft.fft(filtered[0] + 1j * filtered[1], axis=-1) / math.sqrt(CHANNELS)
        real_part = jnp.real(spectrum)
        imag_part = jnp.imag(spectrum)
        knots_now = delay_knots[:, :, segs].astype(jnp.float32)
        knots_prev = delay_knots[:, :, jnp.maximum(segs - 1, 0)].astype(jnp.float32)
        track = (1.0 - weights) * knots_prev[..., None] + weights * knots_now[..., None]
        track = track.reshape(2, STATIONS, frames_dump)
        angle = (2.0 * math.pi * track[0])[..., None] * freq + track[1][..., None]
        cosine = jnp.cos(angle)
        sine = jnp.sin(angle)
        rot_real = (real_part * cosine - imag_part * sine).astype(jnp.bfloat16)
        rot_imag = (real_part * sine + imag_part * cosine).astype(jnp.bfloat16)
        stacked = jnp.stack([rot_real, rot_imag])[..., owner_map].astype(jnp.float32)
        prods = jnp.einsum('psfc,qtfc->pqcst', stacked, stacked, precision=lax.Precision.HIGHEST)
        vis_real = prods[0, 0] + prods[1, 1]
        vis_imag = prods[1, 0] - prods[0, 1]
        result = jnp.stack([vis_real, vis_imag]) / frames_dump
        return result.reshape(2, CHANNELS, STATIONS * STATIONS)
    dumps_all = lax.map(one_dump, jnp.arange(DUMPS, dtype=jnp.int32))
    return jnp.moveaxis(dumps_all, 0, 1)
```

```python
import math

import jax
import jax.numpy as jnp
import numpy as np
from jax import lax
from jax.experimental import pallas as pl
from jax.experimental.pallas import tpu as pltpu
from jax.sharding import PartitionSpec as P

TAPS = 4
DUMP_SEGS = 8
LANES = 128
GROUP = 8


def block_matrix(size, scale):
    counter = np.arange(size)
    angle = 2.0 * math.pi / size * (counter[:, None] * counter[None, :] % size)
    w_real = np.cos(angle) * scale
    w_imag = -np.sin(angle) * scale
    return w_real, w_imag


def split_bf16(values):
    high = values.astype(jnp.bfloat16)
    low = (values - high.astype(jnp.float32)).astype(jnp.bfloat16)
    return high, low


def dot(left, right):
    return jnp.dot(left, right, preferred_element_type=jnp.float32)


def spectra_kernel(
    delays_ref, own_ref, tail_ref, taps_ref, w1h_ref, w1l_ref, twist_ref, w2h_ref, w2l_ref,
    e1_ref, e2_ref, out_ref, window, ext, turned_re, turned_im,
):
    frames = out_ref.shape[1]
    radix = taps_ref.shape[1]
    own_rows = frames * radix
    tail_rows = TAPS * radix
    history = TAPS - 1
    rows = frames * GROUP
    half = frames // 2
    base = pl.program_id(0) * GROUP
    lane = lax.broadcasted_iota(jnp.int32, (1, LANES), 1)

    def shift(part, start, count, where):
        row = start // LANES
        turn = start % LANES
        back = (LANES - turn) % LANES
        near = pltpu.roll(window[part, pl.ds(row, count), :], back, 1)
        far = pltpu.roll(window[part, pl.ds(row + 1, count), :], back, 1)
        ext[part, pl.ds(where, count), :] = jnp.where(lane < LANES - turn, near, far)

    def station(index, carry):
        own_delay = delays_ref[0, base + index]
        prev_delay = delays_ref[1, base + index]
        for part in range(2):
            window[part, 0:tail_rows, :] = tail_ref[part, index].astype(jnp.float32)
            window[part, tail_rows : tail_rows + own_rows, :] = own_ref[part, index].astype(jnp.float32)
            shift(part, radix * LANES - prev_delay, history * radix, 0)
            for frame in range(0, frames, 2):
                shift(
                    part,
                    tail_rows * LANES - own_delay + frame * radix * LANES,
                    2 * radix,
                    (history + frame) * radix,
                )

        def filtered(part, frame):
            total = taps_ref[0] * ext[part, frame * radix : (frame + 1) * radix, :]
            for tap in range(1, TAPS):
                spot = (frame + tap) * radix
                total = total + taps_ref[tap] * ext[part, spot : spot + radix, :]
            return total

        columns = []
        for side in range(2):
            columns.append(
                jnp.concatenate(
                    [filtered(part, side * half + f) for f in range(half) for part in range(2)], axis=0
                )
            )
        high, low = split_bf16(jnp.concatenate(columns, axis=1))
        first = dot(w1h_ref[...], high) + dot(w1h_ref[...], low) + dot(w1l_ref[...], high)
        for side in range(2):
            for f in range(half):
                cols = slice(side * LANES, (side + 1) * LANES)
                real = first[2 * f * radix : (2 * f + 1) * radix, cols]
                imag = first[(2 * f + 1) * radix : (2 * f + 2) * radix, cols]
                place = pl.ds((side * half + f) * GROUP + index, radix, stride=rows)
                turned_re[place, :] = real * twist_ref[0] - imag * twist_ref[1]
                turned_im[place, :] = real * twist_ref[1] + imag * twist_ref[0]
        return carry

    lax.fori_loop(0, GROUP, station, 0)
    batch = 8
    e2_cos = e2_ref[0].reshape(rows, LANES)
    e2_sin = e2_ref[1].reshape(rows, LANES)
    e1_cos = e1_ref[0].reshape(rows, radix)
    e1_sin = e1_ref[1].reshape(rows, radix)
    for start in range(0, radix, batch):
        block = slice(start * rows, (start + batch) * rows)
        high, low = split_bf16(jnp.concatenate([turned_re[block, :], turned_im[block, :]], axis=1))
        second = dot(high, w2h_ref[...]) + dot(low, w2h_ref[...]) + dot(high, w2l_ref[...])
        for step in range(batch):
            c1 = start + step
            real = second[step * rows : (step + 1) * rows, :LANES]
            imag = second[step * rows : (step + 1) * rows, LANES:]
            one_cos = e1_cos[:, c1 : c1 + 1]
            one_sin = e1_sin[:, c1 : c1 + 1]
            cosine = e2_cos * one_cos - e2_sin * one_sin
            sine = e2_sin * one_cos + e2_cos * one_sin
            cols = slice(c1 * LANES, (c1 + 1) * LANES)
            shape = (frames, GROUP, LANES)
            out_ref[0, :, :, cols] = (real * cosine - imag * sine).reshape(shape).astype(jnp.bfloat16)
            out_ref[1, :, :, cols] = (real * sine + imag * cosine).reshape(shape).astype(jnp.bfloat16)


def reorder_kernel(picked_ref, rot_ref, out_ref):
    channels = rot_ref.shape[1]
    tile = out_ref.shape[2]
    chunk = 512
    total = None
    for start in range(0, channels, chunk):
        counter = lax.broadcasted_iota(jnp.int32, (chunk, tile), 0) + start
        hot = jnp.where(counter == picked_ref[0], 1.0, 0.0).astype(jnp.bfloat16)
        term = dot(rot_ref[:, start : start + chunk], hot)
        total = term if total is None else total + term
    out_ref[0] = total.astype(jnp.bfloat16)


def correlate_kernel(data_ref, out_ref, data, acc):
    segs, parts, frames, stations, tile = data_ref.shape
    count = segs * frames
    for part in range(2):
        data[part] = data_ref[:, part].reshape(count, stations, tile).astype(jnp.float32)
    scale = 1.0 / count
    sub = 8

    for tile_a in range(stations // sub):
        low = tile_a * sub
        width = stations - low

        def one_row(pair, carry):
            mine = [low + 2 * pair, low + 2 * pair + 1]

            def frame_step(f, sums):
                b_re = data[0, f, low:, :]
                b_im = data[1, f, low:, :]
                result = []
                for slot, a in enumerate(mine):
                    a_re = data[0, f, pl.ds(a, 1), :]
                    a_im = data[1, f, pl.ds(a, 1), :]
                    result.append(sums[2 * slot] + (a_re * b_re + a_im * b_im))
                    result.append(sums[2 * slot + 1] + (a_im * b_re - a_re * b_im))
                return tuple(result)

            zero = jnp.zeros((width, tile), jnp.float32)
            sums = lax.fori_loop(0, count, frame_step, (zero,) * 4, unroll=4)
            for slot, a in enumerate(mine):
                place = pl.ds(pl.multiple_of(a * stations + low, 8), width)
                acc[0, place, :] = sums[2 * slot] * scale
                acc[1, place, :] = sums[2 * slot + 1] * scale
            return carry

        lax.fori_loop(0, sub // 2, one_row, 0)
    for a in range(sub, stations):
        for low in range(0, a // sub * sub, sub):
            mirror = pl.ds(low * stations + a, sub, stride=stations)
            spot = a * stations + low
            acc[0, spot : spot + sub, :] = acc[0, mirror, :]
            acc[1, spot : spot + sub, :] = -acc[1, mirror, :]
    for part in range(2):
        for start in range(0, stations * stations, LANES):
            out_ref[part, 0, :, start : start + LANES] = acc[part, start : start + LANES, :].T


def shards(samples, delay_knots, sample_delays, owner_map, filter_taps):
    channels = filter_taps.shape[1]
    stations = samples.shape[1]
    seg_len = samples.shape[2]
    frames = seg_len // channels
    devices = lax.axis_size("row")
    position = lax.axis_index("row")
    radix = channels // LANES
    items = channels // devices
    tail_len = TAPS * channels
    route = [(i, i + 1) for i in range(devices - 1)]
    tail, prev_knots = lax.ppermute((samples[:, :, seg_len - tail_len :], delay_knots), "row", route)
    delays = jnp.stack(
        [
            lax.dynamic_index_in_dim(sample_delays, position, 1, keepdims=False),
            lax.dynamic_index_in_dim(sample_delays, jnp.maximum(position - 1, 0), 1, keepdims=False),
        ]
    )
    knots_own = delay_knots[:, :, 0].astype(jnp.float32)
    knots_prev = jnp.where(position == 0, knots_own, prev_knots[:, :, 0].astype(jnp.float32))
    weights = ((jnp.arange(frames, dtype=jnp.float32) + 1.0) / frames)[:, None]
    track = (1.0 - weights) * knots_prev[:, None] + weights * knots_own[:, None]
    turn = 2.0 * math.pi * track[0][..., None]
    coarse = (jnp.arange(LANES, dtype=jnp.float32) * radix - channels / 2) / channels
    fine = jnp.arange(radix, dtype=jnp.float32) / channels
    angle_two = turn * coarse + track[1][..., None]
    angle_one = turn * fine
    e2 = jnp.stack([jnp.cos(angle_two), jnp.sin(angle_two)])
    e1 = jnp.stack([jnp.cos(angle_one), jnp.sin(angle_one)])

    w_real, w_imag = block_matrix(radix, 1.0)
    section_one = np.block([[w_real, -w_imag], [w_imag, w_real]])
    section_one = np.kron(np.eye(frames // 2), section_one).astype(np.float32)
    w_real, w_imag = block_matrix(LANES, 1.0 / math.sqrt(channels))
    section_two = np.block([[w_real, w_imag], [-w_imag, w_real]]).astype(np.float32)
    w1h = section_one.astype(jnp.bfloat16)
    w1l = (section_one - w1h.astype(np.float32)).astype(jnp.bfloat16)
    w2h = section_two.astype(jnp.bfloat16)
    w2l = (section_two - w2h.astype(np.float32)).astype(jnp.bfloat16)
    twist = 2.0 * math.pi / channels * (np.arange(radix)[:, None] * np.arange(LANES)[None, :])
    twist = np.stack([np.cos(twist), -np.sin(twist)]).astype(np.float32)

    rows = frames * GROUP
    whole = lambda *shape: pl.BlockSpec(shape, lambda g: (0,) * len(shape))
    rotated = pl.pallas_call(
        spectra_kernel,
        grid=(stations // GROUP,),
        in_specs=[
            pl.BlockSpec(memory_space=pltpu.SMEM),
            pl.BlockSpec((2, GROUP, frames * radix, LANES), lambda g: (0, g, 0, 0)),
            pl.BlockSpec((2, GROUP, TAPS * radix, LANES), lambda g: (0, g, 0, 0)),
            whole(TAPS, radix, LANES),
            whole(*w1h.shape),
            whole(*w1l.shape),
            whole(2, radix, LANES),
            whole(*w2h.shape),
            whole(*w2l.shape),
            pl.BlockSpec((2, frames, GROUP, radix), lambda g: (0, 0, g, 0)),
            pl.BlockSpec((2, frames, GROUP, LANES), lambda g: (0, 0, g, 0)),
        ],
        out_specs=pl.BlockSpec((2, frames, GROUP, channels), lambda g: (0, 0, g, 0)),
        out_shape=jax.ShapeDtypeStruct((2, frames, stations, channels), jnp.bfloat16),
        scratch_shapes=[
            pltpu.VMEM((2, (frames + TAPS) * radix + 8, LANES), jnp.float32),
            pltpu.VMEM((2, (frames + TAPS - 1) * radix, LANES), jnp.float32),
            pltpu.VMEM((radix * rows, LANES), jnp.float32),
            pltpu.VMEM((radix * rows, LANES), jnp.float32),
        ],
        compiler_params=pltpu.CompilerParams(vmem_limit_bytes=40 * 2**20),
    )(
        delays,
        samples.reshape(2, stations, frames * radix, LANES),
        tail.reshape(2, stations, TAPS * radix, LANES),
        filter_taps.reshape(TAPS, radix, LANES),
        w1h, w1l, twist, w2h, w2l, e1, e2,
    )

    lines = 2 * frames * stations
    picked = (owner_map % radix * LANES + owner_map // radix).reshape(devices, 1, items)
    packed = pl.pallas_call(
        reorder_kernel,
        grid=(devices,),
        in_specs=[
            pl.BlockSpec((1, 1, items), lambda d: (d, 0, 0)),
            pl.BlockSpec((lines, channels), lambda d: (0, 0)),
        ],
        out_specs=pl.BlockSpec((1, lines, items), lambda d: (d, 0, 0)),
        out_shape=jax.ShapeDtypeStruct((devices, lines, items), jnp.bfloat16),
        compiler_params=pltpu.CompilerParams(vmem_limit_bytes=40 * 2**20),
    )(picked, rotated.reshape(lines, channels))

    received = lax.all_to_all(packed, "row", split_axis=0, concat_axis=0, tiled=True)
    received = received.reshape(devices, 2, frames, stations, items)
    dump_count = devices // DUMP_SEGS
    tile = min(LANES, items)
    return pl.pallas_call(
        correlate_kernel,
        grid=(dump_count, items // tile),
        in_specs=[
            pl.BlockSpec((DUMP_SEGS, 2, frames, stations, tile), lambda g, m: (g, 0, 0, 0, m)),
        ],
        out_specs=pl.BlockSpec((2, 1, tile, stations * stations), lambda g, m: (0, g, m, 0)),
        out_shape=jax.ShapeDtypeStruct((2, dump_count, items, stations * stations), jnp.float32),
        scratch_shapes=[
            pltpu.VMEM((2, DUMP_SEGS * frames, stations, tile), jnp.float32),
            pltpu.VMEM((2, stations * stations, tile), jnp.float32),
        ],
        compiler_params=pltpu.CompilerParams(vmem_limit_bytes=40 * 2**20),
    )(received)


def solution(mesh):
    placed = (P(None, "groups", "row"), P(None, "groups", "row"), P("groups", None), P(), P())
    return jax.shard_map(
        shards,
        mesh=mesh,
        in_specs=placed,
        out_specs=P(None, "groups", "row", None),
        check_vma=False,
    )
```

```python
import math
from functools import partial

import jax
import jax.numpy as jnp
import numpy as np
from jax import lax
from jax.experimental import pallas as pl
from jax.experimental.pallas import tpu as pltpu
from jax.sharding import PartitionSpec as P

TAPS = 4
DUMP_SEGS = 8
LANES = 128
GROUP = 8
SUB = 8


def block_matrix(size, scale):
    counter = np.arange(size)
    angle = 2.0 * math.pi / size * (counter[:, None] * counter[None, :] % size)
    w_real = np.cos(angle) * scale
    w_imag = -np.sin(angle) * scale
    return w_real, w_imag


def split_bf16(values):
    high = values.astype(jnp.bfloat16)
    low = (values - high.astype(jnp.float32)).astype(jnp.bfloat16)
    return high, low


def dot(left, right):
    return jnp.dot(left, right, preferred_element_type=jnp.float32)


def spectra_kernel(
    which, delays_ref, own_ref, tail_ref, taps_ref, w1h_ref, w1l_ref, twist_ref, w2h_ref, w2l_ref,
    e1_ref, e2_ref, out_ref, window, ext, turned_re, turned_im,
):
    frames = out_ref.shape[1]
    radix = taps_ref.shape[1]
    own_rows = frames * radix
    tail_rows = TAPS * radix
    history = TAPS - 1
    rows = frames * GROUP
    half = frames // 2
    base = pl.program_id(0) * GROUP
    lane = lax.broadcasted_iota(jnp.int32, (1, LANES), 1)

    def shift(part, start, count, where):
        row = start // LANES
        turn = start % LANES
        back = (LANES - turn) % LANES
        near = pltpu.roll(window[part, pl.ds(row, count), :], back, 1)
        far = pltpu.roll(window[part, pl.ds(row + 1, count), :], back, 1)
        ext[part, pl.ds(where, count), :] = jnp.where(lane < LANES - turn, near, far)

    def station(index, carry):
        own_delay = delays_ref[0, base + index]
        prev_delay = delays_ref[which, base + index]
        for part in range(2):
            window[part, 0:tail_rows, :] = tail_ref[part, index].astype(jnp.float32)
            window[part, tail_rows : tail_rows + own_rows, :] = own_ref[part, index].astype(jnp.float32)
            shift(part, radix * LANES - prev_delay, history * radix, 0)
            for frame in range(0, frames, 2):
                shift(
                    part,
                    tail_rows * LANES - own_delay + frame * radix * LANES,
                    2 * radix,
                    (history + frame) * radix,
                )

        def filtered(part, frame):
            total = taps_ref[0] * ext[part, frame * radix : (frame + 1) * radix, :]
            for tap in range(1, TAPS):
                spot = (frame + tap) * radix
                total = total + taps_ref[tap] * ext[part, spot : spot + radix, :]
            return total

        columns = []
        for side in range(2):
            columns.append(
                jnp.concatenate(
                    [filtered(part, side * half + f) for f in range(half) for part in range(2)], axis=0
                )
            )
        high, low = split_bf16(jnp.concatenate(columns, axis=1))
        first = dot(w1h_ref[...], high) + dot(w1h_ref[...], low) + dot(w1l_ref[...], high)
        for side in range(2):
            for f in range(half):
                cols = slice(side * LANES, (side + 1) * LANES)
                real = first[2 * f * radix : (2 * f + 1) * radix, cols]
                imag = first[(2 * f + 1) * radix : (2 * f + 2) * radix, cols]
                place = pl.ds((side * half + f) * GROUP + index, radix, stride=rows)
                turned_re[place, :] = real * twist_ref[0] - imag * twist_ref[1]
                turned_im[place, :] = real * twist_ref[1] + imag * twist_ref[0]
        return carry

    lax.fori_loop(0, GROUP, station, 0)
    batch = 8
    e2_cos = e2_ref[0].reshape(rows, LANES)
    e2_sin = e2_ref[1].reshape(rows, LANES)
    e1_cos = e1_ref[0].reshape(rows, radix)
    e1_sin = e1_ref[1].reshape(rows, radix)
    for start in range(0, radix, batch):
        block = slice(start * rows, (start + batch) * rows)
        high, low = split_bf16(jnp.concatenate([turned_re[block, :], turned_im[block, :]], axis=1))
        second = dot(high, w2h_ref[...]) + dot(low, w2h_ref[...]) + dot(high, w2l_ref[...])
        for step in range(batch):
            c1 = start + step
            real = second[step * rows : (step + 1) * rows, :LANES]
            imag = second[step * rows : (step + 1) * rows, LANES:]
            one_cos = e1_cos[:, c1 : c1 + 1]
            one_sin = e1_sin[:, c1 : c1 + 1]
            cosine = e2_cos * one_cos - e2_sin * one_sin
            sine = e2_sin * one_cos + e2_cos * one_sin
            cols = slice(c1 * LANES, (c1 + 1) * LANES)
            shape = (frames, GROUP, LANES)
            out_ref[0, :, :, cols] = (real * cosine - imag * sine).reshape(shape).astype(jnp.bfloat16)
            out_ref[1, :, :, cols] = (real * sine + imag * cosine).reshape(shape).astype(jnp.bfloat16)


def reorder_kernel(picked_ref, early_ref, late_ref, out_ref):
    lines, channels = early_ref.shape
    tile = out_ref.shape[2]
    chunk = 512
    totals = [None, None]
    for start in range(0, channels, chunk):
        counter = lax.broadcasted_iota(jnp.int32, (chunk, tile), 0) + start
        hot = jnp.where(counter == picked_ref[0], 1.0, 0.0).astype(jnp.bfloat16)
        for side, ref in enumerate((early_ref, late_ref)):
            term = dot(ref[:, start : start + chunk], hot)
            totals[side] = term if totals[side] is None else totals[side] + term
    out_ref[0, :lines] = totals[0].astype(jnp.bfloat16)
    out_ref[0, lines:] = totals[1].astype(jnp.bfloat16)


def correlate_kernel(data_ref, out_ref, data, acc):
    segs, halves, parts, frames, stations, tile = data_ref.shape
    count = segs * halves * frames
    part_count = segs * frames
    for part in range(2):
        for side in range(halves):
            block = data_ref[:, side, part].reshape(part_count, stations, tile)
            data[part, side * part_count : (side + 1) * part_count] = block.astype(jnp.float32)
    scale = 1.0 / count

    for tile_a in range(stations // SUB):
        low = tile_a * SUB
        width = stations - low

        def one_row(pair, carry):
            mine = [low + 2 * pair, low + 2 * pair + 1]

            def frame_step(f, sums):
                b_re = data[0, f, low:, :]
                b_im = data[1, f, low:, :]
                result = []
                for slot, a in enumerate(mine):
                    a_re = data[0, f, pl.ds(a, 1), :]
                    a_im = data[1, f, pl.ds(a, 1), :]
                    result.append(sums[2 * slot] + (a_re * b_re + a_im * b_im))
                    result.append(sums[2 * slot + 1] + (a_im * b_re - a_re * b_im))
                return tuple(result)

            zero = jnp.zeros((width, tile), jnp.float32)
            sums = lax.fori_loop(0, count, frame_step, (zero,) * 4, unroll=4)
            for slot, a in enumerate(mine):
                place = pl.ds(pl.multiple_of(a * stations + low, 8), width)
                acc[0, place, :] = sums[2 * slot] * scale
                acc[1, place, :] = sums[2 * slot + 1] * scale
            return carry

        lax.fori_loop(0, SUB // 2, one_row, 0)
    diagonal = acc[0, pl.ds(0, stations, stride=stations + 1), :]
    line = lax.broadcasted_iota(jnp.int32, (SUB, tile), 0)
    for a in range(stations):
        own = a // SUB * SUB
        for low in range(0, own, SUB):
            spot = a * stations + low
            acc[0, spot : spot + SUB, :] = -acc[1, pl.ds(low * stations + a, SUB, stride=stations), :]
        spot = slice(a * stations + own, a * stations + own + SUB)
        acc[0, spot, :] = jnp.where(line + own >= a, acc[0, spot, :], acc[1, spot, :])
    pairs = stations * stations
    out_ref[0, :pairs, :] = acc[0].astype(jnp.bfloat16)
    out_ref[0, pairs:, :] = split_bf16(diagonal)[1]


def spread_kernel(packed_ref, out_ref, packed, acc):
    tile = packed_ref.shape[2]
    pairs = acc.shape[1]
    stations = packed_ref.shape[1] - pairs
    packed[...] = packed_ref[0].astype(jnp.float32)
    line = lax.broadcasted_iota(jnp.int32, (SUB, tile), 0)
    for a in range(stations):
        for low in range(0, stations, SUB):
            spot = slice(a * stations + low, a * stations + low + SUB)
            direct = packed[spot, :]
            mirror = packed[pl.ds(low * stations + a, SUB, stride=stations), :]
            if low > a:
                real, imag = direct, -mirror
            elif low + SUB <= a:
                real, imag = mirror, direct
            else:
                fix = packed[pairs + a : pairs + a + 1, :]
                b = line + low
                real = jnp.where(b >= a, direct, mirror) + jnp.where(b == a, fix, 0.0)
                imag = jnp.where(b < a, direct, jnp.where(b == a, 0.0, -mirror))
            acc[0, spot, :] = real
            acc[1, spot, :] = imag
    for part in range(2):
        for start in range(0, pairs, LANES):
            out_ref[part, 0, :, start : start + LANES] = acc[part, start : start + LANES, :].T


def shards(samples, delay_knots, sample_delays, owner_map, filter_taps):
    channels = filter_taps.shape[1]
    stations = samples.shape[1]
    seg_len = samples.shape[2]
    frames = seg_len // channels
    devices = lax.axis_size("row")
    position = lax.axis_index("row")
    radix = channels // LANES
    items = channels // devices
    tail_len = TAPS * channels
    route = [(i, i + 1) for i in range(devices - 1)]
    tail, prev_knots = lax.ppermute((samples[:, :, seg_len - tail_len :], delay_knots), "row", route)
    delays = jnp.stack(
        [
            lax.dynamic_index_in_dim(sample_delays, position, 1, keepdims=False),
            lax.dynamic_index_in_dim(sample_delays, jnp.maximum(position - 1, 0), 1, keepdims=False),
        ]
    )
    knots_own = delay_knots[:, :, 0].astype(jnp.float32)
    knots_prev = jnp.where(position == 0, knots_own, prev_knots[:, :, 0].astype(jnp.float32))
    weights = ((jnp.arange(frames, dtype=jnp.float32) + 1.0) / frames)[:, None]
    track = (1.0 - weights) * knots_prev[:, None] + weights * knots_own[:, None]
    turn = 2.0 * math.pi * track[0][..., None]
    coarse = (jnp.arange(LANES, dtype=jnp.float32) * radix - channels / 2) / channels
    fine = jnp.arange(radix, dtype=jnp.float32) / channels
    angle_two = turn * coarse + track[1][..., None]
    angle_one = turn * fine
    e2 = jnp.stack([jnp.cos(angle_two), jnp.sin(angle_two)])
    e1 = jnp.stack([jnp.cos(angle_one), jnp.sin(angle_one)])

    w_real, w_imag = block_matrix(radix, 1.0)
    section_one = np.block([[w_real, -w_imag], [w_imag, w_real]])
    section_one = np.kron(np.eye(frames // 4), section_one).astype(np.float32)
    w_real, w_imag = block_matrix(LANES, 1.0 / math.sqrt(channels))
    section_two = np.block([[w_real, w_imag], [-w_imag, w_real]]).astype(np.float32)
    w1h = section_one.astype(jnp.bfloat16)
    w1l = (section_one - w1h.astype(np.float32)).astype(jnp.bfloat16)
    w2h = section_two.astype(jnp.bfloat16)
    w2l = (section_two - w2h.astype(np.float32)).astype(jnp.bfloat16)
    twist = 2.0 * math.pi / channels * (np.arange(radix)[:, None] * np.arange(LANES)[None, :])
    twist = np.stack([np.cos(twist), -np.sin(twist)]).astype(np.float32)

    part_frames = frames // 2
    rows = part_frames * GROUP
    part_rows = part_frames * radix
    whole = lambda *shape: pl.BlockSpec(shape, lambda g: (0,) * len(shape))
    blocks = samples.reshape(2, stations, frames * radix, LANES)
    taps = filter_taps.reshape(TAPS, radix, LANES)

    def spectra(side, history, which):
        return pl.pallas_call(
            partial(spectra_kernel, which),
            grid=(stations // GROUP,),
            in_specs=[
                pl.BlockSpec(memory_space=pltpu.SMEM),
                pl.BlockSpec((2, GROUP, part_rows, LANES), lambda g: (0, g, side, 0)),
                pl.BlockSpec((2, GROUP, TAPS * radix, LANES), lambda g: (0, g, 0, 0)),
                whole(TAPS, radix, LANES),
                whole(*w1h.shape),
                whole(*w1l.shape),
                whole(2, radix, LANES),
                whole(*w2h.shape),
                whole(*w2l.shape),
                pl.BlockSpec((2, part_frames, GROUP, radix), lambda g: (0, side, g, 0)),
                pl.BlockSpec((2, part_frames, GROUP, LANES), lambda g: (0, side, g, 0)),
            ],
            out_specs=pl.BlockSpec((2, part_frames, GROUP, channels), lambda g: (0, 0, g, 0)),
            out_shape=jax.ShapeDtypeStruct((2, part_frames, stations, channels), jnp.bfloat16),
            scratch_shapes=[
                pltpu.VMEM((2, (part_frames + TAPS) * radix + 8, LANES), jnp.float32),
                pltpu.VMEM((2, (part_frames + TAPS - 1) * radix, LANES), jnp.float32),
                pltpu.VMEM((radix * rows, LANES), jnp.float32),
                pltpu.VMEM((radix * rows, LANES), jnp.float32),
            ],
            compiler_params=pltpu.CompilerParams(vmem_limit_bytes=40 * 2**20),
            cost_estimate=pl.CostEstimate(
                flops=8 * 10**9, bytes_accessed=8 * 2**20, transcendentals=0
            ),
        )(delays, blocks, history, taps, w1h, w1l, twist, w2h, w2l, e1, e2)

    lines = frames * stations
    late = spectra(1, blocks, 0).reshape(lines, channels)
    early = spectra(0, tail.reshape(2, stations, TAPS * radix, LANES), 1).reshape(lines, channels)

    members = DUMP_SEGS
    dump_count = devices // members
    share = items * dump_count
    picked = (owner_map % radix * LANES + owner_map // radix).reshape(dump_count, members, items)
    picked = picked.transpose(1, 0, 2).reshape(members, 1, share)
    packed = pl.pallas_call(
        reorder_kernel,
        grid=(members,),
        in_specs=[
            pl.BlockSpec((1, 1, share), lambda d: (d, 0, 0)),
            pl.BlockSpec((lines, channels), lambda d: (0, 0)),
            pl.BlockSpec((lines, channels), lambda d: (0, 0)),
        ],
        out_specs=pl.BlockSpec((1, 2 * lines, share), lambda d: (d, 0, 0)),
        out_shape=jax.ShapeDtypeStruct((members, 2 * lines, share), jnp.bfloat16),
        compiler_params=pltpu.CompilerParams(vmem_limit_bytes=50 * 2**20),
    )(picked, early, late)

    near = [[g * members + i for i in range(members)] for g in range(dump_count)]
    far = [[g * members + i for g in range(dump_count)] for i in range(members)]
    received = lax.all_to_all(
        packed, "row", split_axis=0, concat_axis=0, tiled=True, axis_index_groups=near
    )
    received = received.reshape(members, 2, 2, part_frames, stations, share)
    pairs = stations * stations
    height = pairs + stations
    direct = items % LANES == 0
    owners, width = (dump_count, items) if direct else (1, share)
    per = width // LANES
    products = pl.pallas_call(
        correlate_kernel,
        grid=(share // LANES,),
        in_specs=[
            pl.BlockSpec(
                (members, 2, 2, part_frames, stations, LANES), lambda m: (0, 0, 0, 0, 0, m)
            ),
        ],
        out_specs=pl.BlockSpec((1, height, LANES), lambda m: (m // per, 0, m % per)),
        out_shape=jax.ShapeDtypeStruct((owners, height, width), jnp.bfloat16),
        scratch_shapes=[
            pltpu.VMEM((2, members * frames, stations, LANES), jnp.float32),
            pltpu.VMEM((2, pairs, LANES), jnp.float32),
        ],
        compiler_params=pltpu.CompilerParams(vmem_limit_bytes=40 * 2**20),
    )(received)
    if not direct:
        products = products.reshape(height, dump_count, items).transpose(1, 0, 2)
    gathered = lax.all_to_all(
        products, "row", split_axis=0, concat_axis=0, tiled=True, axis_index_groups=far
    )
    tile = LANES if direct else items
    return pl.pallas_call(
        spread_kernel,
        grid=(dump_count, items // tile),
        in_specs=[pl.BlockSpec((1, height, tile), lambda g, m: (g, 0, m))],
        out_specs=pl.BlockSpec((2, 1, tile, pairs), lambda g, m: (0, g, m, 0)),
        out_shape=jax.ShapeDtypeStruct((2, dump_count, items, pairs), jnp.float32),
        scratch_shapes=[
            pltpu.VMEM((height, tile), jnp.float32),
            pltpu.VMEM((2, pairs, tile), jnp.float32),
        ],
        compiler_params=pltpu.CompilerParams(vmem_limit_bytes=40 * 2**20),
    )(gathered)


def solution(mesh):
    placed = (P(None, "groups", "row"), P(None, "groups", "row"), P("groups", None), P(), P())
    return jax.shard_map(
        shards,
        mesh=mesh,
        in_specs=placed,
        out_specs=P(None, "groups", "row", None),
        check_vma=False,
    )
```

```python
import math
from functools import partial

import jax
import jax.numpy as jnp
import numpy as np
from jax import lax
from jax.experimental import pallas as pl
from jax.experimental.pallas import tpu as pltpu
from jax.sharding import PartitionSpec as P

TAPS = 4
DUMP_SEGS = 8
LANES = 128
GROUP = 8
SUB = 8


def block_matrix(size, scale):
    counter = np.arange(size)
    angle = 2.0 * math.pi / size * (counter[:, None] * counter[None, :] % size)
    w_real = np.cos(angle) * scale
    w_imag = -np.sin(angle) * scale
    return w_real, w_imag


def split_bf16(values):
    high = values.astype(jnp.bfloat16)
    low = (values - high.astype(jnp.float32)).astype(jnp.bfloat16)
    return high, low


def dot(left, right):
    return jnp.dot(left, right, preferred_element_type=jnp.float32)


def spectra_kernel(
    which, delays_ref, own_ref, tail_ref, taps_ref, w1h_ref, w1l_ref, twist_ref, w2h_ref, w2l_ref,
    e1_ref, e2_ref, out_ref, window, ext, turned_re, turned_im,
):
    frames = out_ref.shape[1]
    radix = taps_ref.shape[1]
    own_rows = frames * radix
    tail_rows = TAPS * radix
    history = TAPS - 1
    rows = frames * GROUP
    half = frames // 2
    base = pl.program_id(0) * GROUP
    lane = lax.broadcasted_iota(jnp.int32, (1, LANES), 1)

    def shift(part, start, count, where):
        row = start // LANES
        turn = start % LANES
        back = (LANES - turn) % LANES
        near = pltpu.roll(window[part, pl.ds(row, count), :], back, 1)
        far = pltpu.roll(window[part, pl.ds(row + 1, count), :], back, 1)
        ext[part, pl.ds(where, count), :] = jnp.where(lane < LANES - turn, near, far)

    def station(index, carry):
        own_delay = delays_ref[0, base + index]
        prev_delay = delays_ref[which, base + index]
        for part in range(2):
            window[part, 0:tail_rows, :] = tail_ref[part, index].astype(jnp.float32)
            window[part, tail_rows : tail_rows + own_rows, :] = own_ref[part, index].astype(jnp.float32)
            shift(part, radix * LANES - prev_delay, history * radix, 0)
            for frame in range(0, frames, 2):
                shift(
                    part,
                    tail_rows * LANES - own_delay + frame * radix * LANES,
                    2 * radix,
                    (history + frame) * radix,
                )

        def filtered(part, frame):
            total = taps_ref[0] * ext[part, frame * radix : (frame + 1) * radix, :]
            for tap in range(1, TAPS):
                spot = (frame + tap) * radix
                total = total + taps_ref[tap] * ext[part, spot : spot + radix, :]
            return total

        columns = []
        for side in range(2):
            columns.append(
                jnp.concatenate(
                    [filtered(part, side * half + f) for f in range(half) for part in range(2)], axis=0
                )
            )
        high, low = split_bf16(jnp.concatenate(columns, axis=1))
        first = dot(w1h_ref[...], high) + dot(w1h_ref[...], low) + dot(w1l_ref[...], high)
        for side in range(2):
            for f in range(half):
                cols = slice(side * LANES, (side + 1) * LANES)
                real = first[2 * f * radix : (2 * f + 1) * radix, cols]
                imag = first[(2 * f + 1) * radix : (2 * f + 2) * radix, cols]
                place = pl.ds((side * half + f) * GROUP + index, radix, stride=rows)
                turned_re[place, :] = real * twist_ref[0] - imag * twist_ref[1]
                turned_im[place, :] = real * twist_ref[1] + imag * twist_ref[0]
        return carry

    lax.fori_loop(0, GROUP, station, 0)
    batch = 8
    e2_cos = e2_ref[0].reshape(rows, LANES)
    e2_sin = e2_ref[1].reshape(rows, LANES)
    e1_cos = e1_ref[0].reshape(rows, radix)
    e1_sin = e1_ref[1].reshape(rows, radix)
    for start in range(0, radix, batch):
        block = slice(start * rows, (start + batch) * rows)
        high, low = split_bf16(jnp.concatenate([turned_re[block, :], turned_im[block, :]], axis=1))
        second = dot(high, w2h_ref[...]) + dot(low, w2h_ref[...]) + dot(high, w2l_ref[...])
        for step in range(batch):
            c1 = start + step
            real = second[step * rows : (step + 1) * rows, :LANES]
            imag = second[step * rows : (step + 1) * rows, LANES:]
            one_cos = e1_cos[:, c1 : c1 + 1]
            one_sin = e1_sin[:, c1 : c1 + 1]
            cosine = e2_cos * one_cos - e2_sin * one_sin
            sine = e2_sin * one_cos + e2_cos * one_sin
            cols = slice(c1 * LANES, (c1 + 1) * LANES)
            shape = (frames, GROUP, LANES)
            out_ref[0, :, :, cols] = (real * cosine - imag * sine).reshape(shape).astype(jnp.bfloat16)
            out_ref[1, :, :, cols] = (real * sine + imag * cosine).reshape(shape).astype(jnp.bfloat16)


def reorder_kernel(picked_ref, early_ref, late_ref, out_ref):
    lines, channels = early_ref.shape
    tile = out_ref.shape[2]
    chunk = 512
    totals = [None, None]
    for start in range(0, channels, chunk):
        counter = lax.broadcasted_iota(jnp.int32, (chunk, tile), 0) + start
        hot = jnp.where(counter == picked_ref[0], 1.0, 0.0).astype(jnp.bfloat16)
        for side, ref in enumerate((early_ref, late_ref)):
            term = dot(ref[:, start : start + chunk], hot)
            totals[side] = term if totals[side] is None else totals[side] + term
    out_ref[0, :lines] = totals[0].astype(jnp.bfloat16)
    out_ref[0, lines:] = totals[1].astype(jnp.bfloat16)


def correlate_kernel(data_ref, out_ref, data, acc):
    segs, halves, parts, frames, stations, tile = data_ref.shape
    count = segs * halves * frames
    part_count = segs * frames
    for part in range(2):
        for side in range(halves):
            block = data_ref[:, side, part].reshape(part_count, stations, tile)
            data[part, side * part_count : (side + 1) * part_count] = block.astype(jnp.float32)
    scale = 1.0 / count

    for tile_a in range(stations // SUB):
        low = tile_a * SUB
        width = stations - low

        def one_row(pair, carry):
            mine = [low + 2 * pair, low + 2 * pair + 1]

            def frame_step(f, sums):
                b_re = data[0, f, low:, :]
                b_im = data[1, f, low:, :]
                result = []
                for slot, a in enumerate(mine):
                    a_re = data[0, f, pl.ds(a, 1), :]
                    a_im = data[1, f, pl.ds(a, 1), :]
                    result.append(sums[2 * slot] + (a_re * b_re + a_im * b_im))
                    result.append(sums[2 * slot + 1] + (a_im * b_re - a_re * b_im))
                return tuple(result)

            zero = jnp.zeros((width, tile), jnp.float32)
            sums = lax.fori_loop(0, count, frame_step, (zero,) * 4, unroll=4)
            for slot, a in enumerate(mine):
                place = pl.ds(pl.multiple_of(a * stations + low, 8), width)
                acc[0, place, :] = sums[2 * slot] * scale
                acc[1, place, :] = sums[2 * slot + 1] * scale
            return carry

        lax.fori_loop(0, SUB // 2, one_row, 0)
    diagonal = acc[0, pl.ds(0, stations, stride=stations + 1), :]
    line = lax.broadcasted_iota(jnp.int32, (SUB, tile), 0)
    for a in range(stations):
        own = a // SUB * SUB
        for low in range(0, own, SUB):
            spot = a * stations + low
            acc[0, spot : spot + SUB, :] = -acc[1, pl.ds(low * stations + a, SUB, stride=stations), :]
        spot = slice(a * stations + own, a * stations + own + SUB)
        acc[0, spot, :] = jnp.where(line + own >= a, acc[0, spot, :], acc[1, spot, :])
    pairs = stations * stations
    out_ref[0, :pairs, :] = acc[0].astype(jnp.bfloat16)
    out_ref[0, pairs:, :] = split_bf16(diagonal)[1]


def spread_kernel(own_ref, packed_ref, out_ref, packed, acc):
    tile = packed_ref.shape[2]
    pairs = acc.shape[1]
    stations = packed_ref.shape[1] - pairs
    packed[...] = packed_ref[0].astype(jnp.float32)
    line = lax.broadcasted_iota(jnp.int32, (SUB, tile), 0)
    for a in range(stations):
        for low in range(0, stations, SUB):
            spot = slice(a * stations + low, a * stations + low + SUB)
            direct = packed[spot, :]
            mirror = packed[pl.ds(low * stations + a, SUB, stride=stations), :]
            if low > a:
                real, imag = direct, -mirror
            elif low + SUB <= a:
                real, imag = mirror, direct
            else:
                fix = packed[pairs + a : pairs + a + 1, :]
                b = line + low
                real = jnp.where(b >= a, direct, mirror) + jnp.where(b == a, fix, 0.0)
                imag = jnp.where(b < a, direct, jnp.where(b == a, 0.0, -mirror))
            acc[0, spot, :] = real
            acc[1, spot, :] = imag
    for part in range(2):
        for start in range(0, pairs, LANES):
            out_ref[part, 0, :, start : start + LANES] = acc[part, start : start + LANES, :].T


def shards(samples, delay_knots, sample_delays, owner_map, filter_taps):
    channels = filter_taps.shape[1]
    stations = samples.shape[1]
    seg_len = samples.shape[2]
    frames = seg_len // channels
    devices = lax.axis_size("row")
    position = lax.axis_index("row")
    radix = channels // LANES
    items = channels // devices
    tail_len = TAPS * channels
    route = [(i, i + 1) for i in range(devices - 1)]
    tail, prev_knots = lax.ppermute((samples[:, :, seg_len - tail_len :], delay_knots), "row", route)
    delays = jnp.stack(
        [
            lax.dynamic_index_in_dim(sample_delays, position, 1, keepdims=False),
            lax.dynamic_index_in_dim(sample_delays, jnp.maximum(position - 1, 0), 1, keepdims=False),
        ]
    )
    knots_own = delay_knots[:, :, 0].astype(jnp.float32)
    knots_prev = jnp.where(position == 0, knots_own, prev_knots[:, :, 0].astype(jnp.float32))
    weights = ((jnp.arange(frames, dtype=jnp.float32) + 1.0) / frames)[:, None]
    track = (1.0 - weights) * knots_prev[:, None] + weights * knots_own[:, None]
    turn = 2.0 * math.pi * track[0][..., None]
    coarse = (jnp.arange(LANES, dtype=jnp.float32) * radix - channels / 2) / channels
    fine = jnp.arange(radix, dtype=jnp.float32) / channels
    angle_two = turn * coarse + track[1][..., None]
    angle_one = turn * fine
    e2 = jnp.stack([jnp.cos(angle_two), jnp.sin(angle_two)])
    e1 = jnp.stack([jnp.cos(angle_one), jnp.sin(angle_one)])

    w_real, w_imag = block_matrix(radix, 1.0)
    section_one = np.block([[w_real, -w_imag], [w_imag, w_real]])
    section_one = np.kron(np.eye(frames // 4), section_one).astype(np.float32)
    w_real, w_imag = block_matrix(LANES, 1.0 / math.sqrt(channels))
    section_two = np.block([[w_real, w_imag], [-w_imag, w_real]]).astype(np.float32)
    w1h = section_one.astype(jnp.bfloat16)
    w1l = (section_one - w1h.astype(np.float32)).astype(jnp.bfloat16)
    w2h = section_two.astype(jnp.bfloat16)
    w2l = (section_two - w2h.astype(np.float32)).astype(jnp.bfloat16)
    twist = 2.0 * math.pi / channels * (np.arange(radix)[:, None] * np.arange(LANES)[None, :])
    twist = np.stack([np.cos(twist), -np.sin(twist)]).astype(np.float32)

    part_frames = frames // 2
    rows = part_frames * GROUP
    part_rows = part_frames * radix
    whole = lambda *shape: pl.BlockSpec(shape, lambda g: (0,) * len(shape))
    blocks = samples.reshape(2, stations, frames * radix, LANES)
    taps = filter_taps.reshape(TAPS, radix, LANES)

    def spectra(side, history, which):
        return pl.pallas_call(
            partial(spectra_kernel, which),
            grid=(stations // GROUP,),
            in_specs=[
                pl.BlockSpec(memory_space=pltpu.SMEM),
                pl.BlockSpec((2, GROUP, part_rows, LANES), lambda g: (0, g, side, 0)),
                pl.BlockSpec((2, GROUP, TAPS * radix, LANES), lambda g: (0, g, 0, 0)),
                whole(TAPS, radix, LANES),
                whole(*w1h.shape),
                whole(*w1l.shape),
                whole(2, radix, LANES),
                whole(*w2h.shape),
                whole(*w2l.shape),
                pl.BlockSpec((2, part_frames, GROUP, radix), lambda g: (0, side, g, 0)),
                pl.BlockSpec((2, part_frames, GROUP, LANES), lambda g: (0, side, g, 0)),
            ],
            out_specs=pl.BlockSpec((2, part_frames, GROUP, channels), lambda g: (0, 0, g, 0)),
            out_shape=jax.ShapeDtypeStruct((2, part_frames, stations, channels), jnp.bfloat16),
            scratch_shapes=[
                pltpu.VMEM((2, (part_frames + TAPS) * radix + 8, LANES), jnp.float32),
                pltpu.VMEM((2, (part_frames + TAPS - 1) * radix, LANES), jnp.float32),
                pltpu.VMEM((radix * rows, LANES), jnp.float32),
                pltpu.VMEM((radix * rows, LANES), jnp.float32),
            ],
            compiler_params=pltpu.CompilerParams(vmem_limit_bytes=40 * 2**20),
            cost_estimate=pl.CostEstimate(
                flops=8 * 10**9, bytes_accessed=8 * 2**20, transcendentals=0
            ),
        )(delays, blocks, history, taps, w1h, w1l, twist, w2h, w2l, e1, e2)

    lines = frames * stations
    late = spectra(1, blocks, 0).reshape(lines, channels)
    early = spectra(0, tail.reshape(2, stations, TAPS * radix, LANES), 1).reshape(lines, channels)

    members = DUMP_SEGS
    dump_count = devices // members
    share = items * dump_count
    picked = (owner_map % radix * LANES + owner_map // radix).reshape(dump_count, members, items)
    mine = position // members
    picked = jnp.roll(picked, -mine, axis=0)
    picked = picked.transpose(1, 0, 2).reshape(members, 1, share)
    packed = pl.pallas_call(
        reorder_kernel,
        grid=(members,),
        in_specs=[
            pl.BlockSpec((1, 1, share), lambda d: (d, 0, 0)),
            pl.BlockSpec((lines, channels), lambda d: (0, 0)),
            pl.BlockSpec((lines, channels), lambda d: (0, 0)),
        ],
        out_specs=pl.BlockSpec((1, 2 * lines, share), lambda d: (d, 0, 0)),
        out_shape=jax.ShapeDtypeStruct((members, 2 * lines, share), jnp.bfloat16),
        compiler_params=pltpu.CompilerParams(vmem_limit_bytes=50 * 2**20),
    )(picked, early, late)

    near = [[g * members + i for i in range(members)] for g in range(dump_count)]
    received = lax.all_to_all(
        packed, "row", split_axis=0, concat_axis=0, tiled=True, axis_index_groups=near
    )
    received = received.reshape(members, 2, 2, part_frames, stations, share)
    pairs = stations * stations
    height = pairs + stations
    direct = items % LANES == 0
    width = items if direct else share
    per = width // LANES

    def correlate(first):
        return pl.pallas_call(
            correlate_kernel,
            grid=(per,),
            in_specs=[
                pl.BlockSpec(
                    (members, 2, 2, part_frames, stations, LANES),
                    lambda m: (0, 0, 0, 0, 0, first + m),
                ),
            ],
            out_specs=pl.BlockSpec((1, height, LANES), lambda m: (0, 0, m)),
            out_shape=jax.ShapeDtypeStruct((1, height, width), jnp.bfloat16),
            scratch_shapes=[
                pltpu.VMEM((2, members * frames, stations, LANES), jnp.float32),
                pltpu.VMEM((2, pairs, LANES), jnp.float32),
            ],
            compiler_params=pltpu.CompilerParams(vmem_limit_bytes=40 * 2**20),
            cost_estimate=pl.CostEstimate(
                flops=8 * 10**9, bytes_accessed=8 * 2**20, transcendentals=0
            ),
        )(received)

    if not direct:
        everything = correlate(0)
    gathered = [None] * dump_count
    for k in list(range(1, dump_count)) + [0]:
        if direct:
            product = correlate(k * per)
        else:
            product = everything[:, :, k * items : (k + 1) * items]
        if k:
            route = [(i, (i + k * members) % devices) for i in range(devices)]
            product = lax.ppermute(product, "row", route)
        gathered[k] = product
    gathered = jnp.concatenate(gathered, axis=0)
    tile = LANES if direct else items
    return pl.pallas_call(
        spread_kernel,
        grid_spec=pltpu.PrefetchScalarGridSpec(
            num_scalar_prefetch=1,
            grid=(dump_count, items // tile),
            in_specs=[pl.BlockSpec((1, height, tile), lambda k, m, own: (k, 0, m))],
            out_specs=pl.BlockSpec(
                (2, 1, tile, pairs),
                lambda k, m, own: (0, lax.rem(own[0] + dump_count - k, dump_count), m, 0),
            ),
            scratch_shapes=[
                pltpu.VMEM((height, tile), jnp.float32),
                pltpu.VMEM((2, pairs, tile), jnp.float32),
            ],
        ),
        out_shape=jax.ShapeDtypeStruct((2, dump_count, items, pairs), jnp.float32),
        compiler_params=pltpu.CompilerParams(vmem_limit_bytes=40 * 2**20),
    )(jnp.full((1,), mine, jnp.int32), gathered)


def solution(mesh):
    placed = (P(None, "groups", "row"), P(None, "groups", "row"), P("groups", None), P(), P())
    return jax.shard_map(
        shards,
        mesh=mesh,
        in_specs=placed,
        out_specs=P(None, "groups", "row", None),
        check_vma=False,
    )
```

```python
import math
from functools import partial

import jax
import jax.numpy as jnp
import numpy as np
from jax import lax
from jax.experimental import pallas as pl
from jax.experimental.pallas import tpu as pltpu
from jax.sharding import PartitionSpec as P

TAPS = 4
DUMP_SEGS = 8
LANES = 128
GROUP = 8
SUB = 8
ROWS = 4


def block_matrix(size, scale):
    counter = np.arange(size)
    angle = 2.0 * math.pi / size * (counter[:, None] * counter[None, :] % size)
    w_real = np.cos(angle) * scale
    w_imag = -np.sin(angle) * scale
    return w_real, w_imag


def split_bf16(values):
    high = values.astype(jnp.bfloat16)
    low = (values - high.astype(jnp.float32)).astype(jnp.bfloat16)
    return high, low


def dot(left, right):
    return jnp.dot(left, right, preferred_element_type=jnp.float32)


def spectra_kernel(
    which, delays_ref, own_ref, tail_ref, taps_ref, w1h_ref, w1l_ref, twist_ref, w2h_ref, w2l_ref,
    e1_ref, e2_ref, out_ref, window, ext, turned_re, turned_im,
):
    frames = out_ref.shape[1]
    radix = taps_ref.shape[1]
    own_rows = frames * radix
    tail_rows = TAPS * radix
    history = TAPS - 1
    rows = frames * GROUP
    half = frames // 2
    base = pl.program_id(0) * GROUP
    lane = lax.broadcasted_iota(jnp.int32, (1, LANES), 1)

    def shift(spare, part, start, count, where):
        row = start // LANES
        turn = start % LANES
        back = (LANES - turn) % LANES
        near = pltpu.roll(window[spare + part, pl.ds(row, count), :], back, 1)
        far = pltpu.roll(window[spare + part, pl.ds(row + 1, count), :], back, 1)
        ext[spare + part, pl.ds(where, count), :] = jnp.where(lane < LANES - turn, near, far)

    def station(index, spare):
        own_delay = delays_ref[0, base + index]
        prev_delay = delays_ref[which, base + index]
        for part in range(2):
            window[spare + part, 0:tail_rows, :] = tail_ref[part, index].astype(jnp.float32)
            window[spare + part, tail_rows : tail_rows + own_rows, :] = own_ref[part, index].astype(jnp.float32)
            shift(spare, part, radix * LANES - prev_delay, history * radix, 0)
            for frame in range(0, frames, 2):
                shift(
                    spare,
                    part,
                    tail_rows * LANES - own_delay + frame * radix * LANES,
                    2 * radix,
                    (history + frame) * radix,
                )

        def filtered(part, frame):
            total = taps_ref[0] * ext[spare + part, frame * radix : (frame + 1) * radix, :]
            for tap in range(1, TAPS):
                spot = (frame + tap) * radix
                total = total + taps_ref[tap] * ext[spare + part, spot : spot + radix, :]
            return total

        columns = []
        for side in range(2):
            columns.append(
                jnp.concatenate(
                    [filtered(part, side * half + f) for f in range(half) for part in range(2)], axis=0
                )
            )
        high, low = split_bf16(jnp.concatenate(columns, axis=1))
        first = dot(w1h_ref[...], high) + dot(w1h_ref[...], low) + dot(w1l_ref[...], high)
        for side in range(2):
            for f in range(half):
                cols = slice(side * LANES, (side + 1) * LANES)
                real = first[2 * f * radix : (2 * f + 1) * radix, cols]
                imag = first[(2 * f + 1) * radix : (2 * f + 2) * radix, cols]
                place = pl.ds((side * half + f) * GROUP + index, radix, stride=rows)
                turned_re[place, :] = real * twist_ref[0] - imag * twist_ref[1]
                turned_im[place, :] = real * twist_ref[1] + imag * twist_ref[0]

    def two_stations(pair, carry):
        station(2 * pair, 0)
        station(2 * pair + 1, 2)
        return carry

    lax.fori_loop(0, GROUP // 2, two_stations, 0)
    batch = 16
    e2_cos = e2_ref[0].reshape(rows, LANES)
    e2_sin = e2_ref[1].reshape(rows, LANES)
    e1_cos = e1_ref[0].reshape(rows, radix)
    e1_sin = e1_ref[1].reshape(rows, radix)
    for start in range(0, radix, batch):
        block = slice(start * rows, (start + batch) * rows)
        high, low = split_bf16(jnp.concatenate([turned_re[block, :], turned_im[block, :]], axis=1))
        second = dot(high, w2h_ref[...]) + dot(low, w2h_ref[...]) + dot(high, w2l_ref[...])
        for step in range(batch):
            c1 = start + step
            real = second[step * rows : (step + 1) * rows, :LANES]
            imag = second[step * rows : (step + 1) * rows, LANES:]
            one_cos = e1_cos[:, c1 : c1 + 1]
            one_sin = e1_sin[:, c1 : c1 + 1]
            cosine = e2_cos * one_cos - e2_sin * one_sin
            sine = e2_sin * one_cos + e2_cos * one_sin
            cols = slice(c1 * LANES, (c1 + 1) * LANES)
            shape = (frames, GROUP, LANES)
            out_ref[0, :, :, cols] = (real * cosine - imag * sine).reshape(shape).astype(jnp.bfloat16)
            out_ref[1, :, :, cols] = (real * sine + imag * cosine).reshape(shape).astype(jnp.bfloat16)


def reorder_kernel(picked_ref, early_ref, late_ref, out_ref):
    lines, channels = early_ref.shape
    tile = out_ref.shape[2]
    chunk = 512
    totals = [None, None]
    for start in range(0, channels, chunk):
        counter = lax.broadcasted_iota(jnp.int32, (chunk, tile), 0) + start
        hot = jnp.where(counter == picked_ref[0], 1.0, 0.0).astype(jnp.bfloat16)
        for side, ref in enumerate((early_ref, late_ref)):
            term = dot(ref[:, start : start + chunk], hot)
            totals[side] = term if totals[side] is None else totals[side] + term
    out_ref[0, :lines] = totals[0].astype(jnp.bfloat16)
    out_ref[0, lines:] = totals[1].astype(jnp.bfloat16)


def correlate_kernel(data_ref, out_ref, data, acc):
    segs, halves, parts, frames, stations, tile = data_ref.shape
    count = segs * halves * frames
    part_count = segs * frames
    for part in range(2):
        for side in range(halves):
            block = data_ref[:, side, part].reshape(part_count, stations, tile)
            data[part, side * part_count : (side + 1) * part_count] = block.astype(jnp.float32)
    scale = 1.0 / count

    for tile_a in range(stations // SUB):
        low = tile_a * SUB
        width = stations - low

        def one_row(pair, carry):
            mine = [low + ROWS * pair + i for i in range(ROWS)]

            def frame_step(f, sums):
                b_re = data[0, f, low:, :]
                b_im = data[1, f, low:, :]
                result = []
                for slot, a in enumerate(mine):
                    a_re = data[0, f, pl.ds(a, 1), :]
                    a_im = data[1, f, pl.ds(a, 1), :]
                    result.append(sums[2 * slot] + (a_re * b_re + a_im * b_im))
                    result.append(sums[2 * slot + 1] + (a_im * b_re - a_re * b_im))
                return tuple(result)

            zero = jnp.zeros((width, tile), jnp.float32)
            sums = lax.fori_loop(0, count, frame_step, (zero,) * (2 * ROWS), unroll=4)
            for slot, a in enumerate(mine):
                place = pl.ds(pl.multiple_of(a * stations + low, 8), width)
                acc[0, place, :] = sums[2 * slot] * scale
                acc[1, place, :] = sums[2 * slot + 1] * scale
            return carry

        lax.fori_loop(0, SUB // ROWS, one_row, 0)
    diagonal = acc[0, pl.ds(0, stations, stride=stations + 1), :]
    line = lax.broadcasted_iota(jnp.int32, (SUB, tile), 0)
    for a in range(stations):
        own = a // SUB * SUB
        for low in range(0, own, SUB):
            spot = a * stations + low
            acc[0, spot : spot + SUB, :] = -acc[1, pl.ds(low * stations + a, SUB, stride=stations), :]
        spot = slice(a * stations + own, a * stations + own + SUB)
        acc[0, spot, :] = jnp.where(line + own >= a, acc[0, spot, :], acc[1, spot, :])
    pairs = stations * stations
    out_ref[0, :pairs, :] = acc[0].astype(jnp.bfloat16)
    out_ref[0, pairs:, :] = split_bf16(diagonal)[1]


def spread_kernel(own_ref, packed_ref, out_ref, packed, acc):
    tile = packed_ref.shape[2]
    pairs = acc.shape[1]
    stations = packed_ref.shape[1] - pairs
    packed[...] = packed_ref[0].astype(jnp.float32)
    line = lax.broadcasted_iota(jnp.int32, (SUB, tile), 0)
    for a in range(stations):
        for low in range(0, stations, SUB):
            spot = slice(a * stations + low, a * stations + low + SUB)
            direct = packed[spot, :]
            mirror = packed[pl.ds(low * stations + a, SUB, stride=stations), :]
            if low > a:
                real, imag = direct, -mirror
            elif low + SUB <= a:
                real, imag = mirror, direct
            else:
                fix = packed[pairs + a : pairs + a + 1, :]
                b = line + low
                real = jnp.where(b >= a, direct, mirror) + jnp.where(b == a, fix, 0.0)
                imag = jnp.where(b < a, direct, jnp.where(b == a, 0.0, -mirror))
            acc[0, spot, :] = real
            acc[1, spot, :] = imag
    for part in range(2):
        for start in range(0, pairs, LANES):
            out_ref[part, 0, :, start : start + LANES] = acc[part, start : start + LANES, :].T


def shards(samples, delay_knots, sample_delays, owner_map, filter_taps):
    channels = filter_taps.shape[1]
    stations = samples.shape[1]
    seg_len = samples.shape[2]
    frames = seg_len // channels
    devices = lax.axis_size("row")
    position = lax.axis_index("row")
    radix = channels // LANES
    items = channels // devices
    tail_len = TAPS * channels
    route = [(i, i + 1) for i in range(devices - 1)]
    tail, prev_knots = lax.ppermute((samples[:, :, seg_len - tail_len :], delay_knots), "row", route)
    delays = jnp.stack(
        [
            lax.dynamic_index_in_dim(sample_delays, position, 1, keepdims=False),
            lax.dynamic_index_in_dim(sample_delays, jnp.maximum(position - 1, 0), 1, keepdims=False),
        ]
    )
    knots_own = delay_knots[:, :, 0].astype(jnp.float32)
    knots_prev = jnp.where(position == 0, knots_own, prev_knots[:, :, 0].astype(jnp.float32))
    weights = ((jnp.arange(frames, dtype=jnp.float32) + 1.0) / frames)[:, None]
    track = (1.0 - weights) * knots_prev[:, None] + weights * knots_own[:, None]
    turn = 2.0 * math.pi * track[0][..., None]
    coarse = (jnp.arange(LANES, dtype=jnp.float32) * radix - channels / 2) / channels
    fine = jnp.arange(radix, dtype=jnp.float32) / channels
    angle_two = turn * coarse + track[1][..., None]
    angle_one = turn * fine
    e2 = jnp.stack([jnp.cos(angle_two), jnp.sin(angle_two)])
    e1 = jnp.stack([jnp.cos(angle_one), jnp.sin(angle_one)])

    w_real, w_imag = block_matrix(radix, 1.0)
    section_one = np.block([[w_real, -w_imag], [w_imag, w_real]])
    section_one = np.kron(np.eye(frames // 4), section_one).astype(np.float32)
    w_real, w_imag = block_matrix(LANES, 1.0 / math.sqrt(channels))
    section_two = np.block([[w_real, w_imag], [-w_imag, w_real]]).astype(np.float32)
    w1h = section_one.astype(jnp.bfloat16)
    w1l = (section_one - w1h.astype(np.float32)).astype(jnp.bfloat16)
    w2h = section_two.astype(jnp.bfloat16)
    w2l = (section_two - w2h.astype(np.float32)).astype(jnp.bfloat16)
    twist = 2.0 * math.pi / channels * (np.arange(radix)[:, None] * np.arange(LANES)[None, :])
    twist = np.stack([np.cos(twist), -np.sin(twist)]).astype(np.float32)

    part_frames = frames // 2
    rows = part_frames * GROUP
    part_rows = part_frames * radix
    whole = lambda *shape: pl.BlockSpec(shape, lambda g: (0,) * len(shape))
    blocks = samples.reshape(2, stations, frames * radix, LANES)
    taps = filter_taps.reshape(TAPS, radix, LANES)

    def spectra(side, history, which):
        return pl.pallas_call(
            partial(spectra_kernel, which),
            grid=(stations // GROUP,),
            in_specs=[
                pl.BlockSpec(memory_space=pltpu.SMEM),
                pl.BlockSpec((2, GROUP, part_rows, LANES), lambda g: (0, g, side, 0)),
                pl.BlockSpec((2, GROUP, TAPS * radix, LANES), lambda g: (0, g, 0, 0)),
                whole(TAPS, radix, LANES),
                whole(*w1h.shape),
                whole(*w1l.shape),
                whole(2, radix, LANES),
                whole(*w2h.shape),
                whole(*w2l.shape),
                pl.BlockSpec((2, part_frames, GROUP, radix), lambda g: (0, side, g, 0)),
                pl.BlockSpec((2, part_frames, GROUP, LANES), lambda g: (0, side, g, 0)),
            ],
            out_specs=pl.BlockSpec((2, part_frames, GROUP, channels), lambda g: (0, 0, g, 0)),
            out_shape=jax.ShapeDtypeStruct((2, part_frames, stations, channels), jnp.bfloat16),
            scratch_shapes=[
                pltpu.VMEM((4, (part_frames + TAPS) * radix + 8, LANES), jnp.float32),
                pltpu.VMEM((4, (part_frames + TAPS - 1) * radix, LANES), jnp.float32),
                pltpu.VMEM((radix * rows, LANES), jnp.float32),
                pltpu.VMEM((radix * rows, LANES), jnp.float32),
            ],
            compiler_params=pltpu.CompilerParams(vmem_limit_bytes=40 * 2**20),
            cost_estimate=pl.CostEstimate(
                flops=8 * 10**9, bytes_accessed=8 * 2**20, transcendentals=0
            ),
        )(delays, blocks, history, taps, w1h, w1l, twist, w2h, w2l, e1, e2)

    lines = frames * stations
    late = spectra(1, blocks, 0).reshape(lines, channels)
    early = spectra(0, tail.reshape(2, stations, TAPS * radix, LANES), 1).reshape(lines, channels)

    members = DUMP_SEGS
    dump_count = devices // members
    share = items * dump_count
    picked = (owner_map % radix * LANES + owner_map // radix).reshape(dump_count, members, items)
    mine = position // members
    picked = jnp.roll(picked, -mine, axis=0)
    picked = picked.transpose(1, 0, 2).reshape(members, 1, share)
    packed = pl.pallas_call(
        reorder_kernel,
        grid=(members,),
        in_specs=[
            pl.BlockSpec((1, 1, share), lambda d: (d, 0, 0)),
            pl.BlockSpec((lines, channels), lambda d: (0, 0)),
            pl.BlockSpec((lines, channels), lambda d: (0, 0)),
        ],
        out_specs=pl.BlockSpec((1, 2 * lines, share), lambda d: (d, 0, 0)),
        out_shape=jax.ShapeDtypeStruct((members, 2 * lines, share), jnp.bfloat16),
        compiler_params=pltpu.CompilerParams(vmem_limit_bytes=50 * 2**20),
    )(picked, early, late)

    near = [[g * members + i for i in range(members)] for g in range(dump_count)]
    received = lax.all_to_all(
        packed, "row", split_axis=0, concat_axis=0, tiled=True, axis_index_groups=near
    )
    received = received.reshape(members, 2, 2, part_frames, stations, share)
    pairs = stations * stations
    height = pairs + stations
    direct = items % LANES == 0
    width = items if direct else share
    per = width // LANES

    def correlate(first):
        return pl.pallas_call(
            correlate_kernel,
            grid=(per,),
            in_specs=[
                pl.BlockSpec(
                    (members, 2, 2, part_frames, stations, LANES),
                    lambda m: (0, 0, 0, 0, 0, first + m),
                ),
            ],
            out_specs=pl.BlockSpec((1, height, LANES), lambda m: (0, 0, m)),
            out_shape=jax.ShapeDtypeStruct((1, height, width), jnp.bfloat16),
            scratch_shapes=[
                pltpu.VMEM((2, members * frames, stations, LANES), jnp.float32),
                pltpu.VMEM((2, pairs, LANES), jnp.float32),
            ],
            compiler_params=pltpu.CompilerParams(vmem_limit_bytes=40 * 2**20),
            cost_estimate=pl.CostEstimate(
                flops=8 * 10**9, bytes_accessed=8 * 2**20, transcendentals=0
            ),
        )(received)

    if not direct:
        everything = correlate(0)
    gathered = [None] * dump_count
    for k in list(range(1, dump_count)) + [0]:
        if direct:
            product = correlate(k * per)
        else:
            product = everything[:, :, k * items : (k + 1) * items]
        if k:
            route = [(i, (i + k * members) % devices) for i in range(devices)]
            product = lax.ppermute(product, "row", route)
        gathered[k] = product
    gathered = jnp.concatenate(gathered, axis=0)
    tile = LANES if direct else items
    return pl.pallas_call(
        spread_kernel,
        grid_spec=pltpu.PrefetchScalarGridSpec(
            num_scalar_prefetch=1,
            grid=(dump_count, items // tile),
            in_specs=[pl.BlockSpec((1, height, tile), lambda k, m, own: (k, 0, m))],
            out_specs=pl.BlockSpec(
                (2, 1, tile, pairs),
                lambda k, m, own: (0, lax.rem(own[0] + dump_count - k, dump_count), m, 0),
            ),
            scratch_shapes=[
                pltpu.VMEM((height, tile), jnp.float32),
                pltpu.VMEM((2, pairs, tile), jnp.float32),
            ],
        ),
        out_shape=jax.ShapeDtypeStruct((2, dump_count, items, pairs), jnp.float32),
        compiler_params=pltpu.CompilerParams(vmem_limit_bytes=40 * 2**20),
    )(jnp.full((1,), mine, jnp.int32), gathered)


def solution(mesh):
    placed = (P(None, "groups", "row"), P(None, "groups", "row"), P("groups", None), P(), P())
    return jax.shard_map(
        shards,
        mesh=mesh,
        in_specs=placed,
        out_specs=P(None, "groups", "row", None),
        check_vma=False,
    )
```

```python
import math
from functools import partial

import jax
import jax.numpy as jnp
import numpy as np
from jax import lax
from jax.experimental import pallas as pl
from jax.experimental.pallas import tpu as pltpu
from jax.sharding import PartitionSpec as P

TAPS = 4
DUMP_SEGS = 8
LANES = 128
GROUP = 8
SUB = 8
ROWS = 4
TOGETHER = 4


def block_matrix(size, scale):
    counter = np.arange(size)
    angle = 2.0 * math.pi / size * (counter[:, None] * counter[None, :] % size)
    w_real = np.cos(angle) * scale
    w_imag = -np.sin(angle) * scale
    return w_real, w_imag


def split_bf16(values):
    high = values.astype(jnp.bfloat16)
    low = (values - high.astype(jnp.float32)).astype(jnp.bfloat16)
    return high, low


def dot(left, right):
    return jnp.dot(left, right, preferred_element_type=jnp.float32)


def spectra_kernel(
    which, delays_ref, own_ref, tail_ref, taps_ref, w1h_ref, w1l_ref, twist_ref, w2h_ref, w2l_ref,
    e1_ref, e2_ref, out_ref, window, ext, turned_re, turned_im,
):
    frames = out_ref.shape[1]
    radix = taps_ref.shape[1]
    own_rows = frames * radix
    tail_rows = TAPS * radix
    history = TAPS - 1
    rows = frames * GROUP
    half = frames // 2
    base = pl.program_id(0) * GROUP
    lane = lax.broadcasted_iota(jnp.int32, (1, LANES), 1)

    def shift(spare, part, start, count, where):
        row = start // LANES
        turn = start % LANES
        back = (LANES - turn) % LANES
        near = pltpu.roll(window[spare + part, pl.ds(row, count), :], back, 1)
        far = pltpu.roll(window[spare + part, pl.ds(row + 1, count), :], back, 1)
        ext[spare + part, pl.ds(where, count), :] = jnp.where(lane < LANES - turn, near, far)

    def station(index, spare):
        own_delay = delays_ref[0, base + index]
        prev_delay = delays_ref[which, base + index]
        for part in range(2):
            window[spare + part, 0:tail_rows, :] = tail_ref[part, index].astype(jnp.float32)
            window[spare + part, tail_rows : tail_rows + own_rows, :] = own_ref[part, index].astype(jnp.float32)
            shift(spare, part, radix * LANES - prev_delay, history * radix, 0)
            for frame in range(0, frames, 2):
                shift(
                    spare,
                    part,
                    tail_rows * LANES - own_delay + frame * radix * LANES,
                    2 * radix,
                    (history + frame) * radix,
                )

        def filtered(part, frame):
            total = taps_ref[0] * ext[spare + part, frame * radix : (frame + 1) * radix, :]
            for tap in range(1, TAPS):
                spot = (frame + tap) * radix
                total = total + taps_ref[tap] * ext[spare + part, spot : spot + radix, :]
            return total

        columns = []
        for side in range(2):
            columns.append(
                jnp.concatenate(
                    [filtered(part, side * half + f) for f in range(half) for part in range(2)], axis=0
                )
            )
        high, low = split_bf16(jnp.concatenate(columns, axis=1))
        first = dot(w1h_ref[...], high) + dot(w1h_ref[...], low) + dot(w1l_ref[...], high)
        for side in range(2):
            for f in range(half):
                cols = slice(side * LANES, (side + 1) * LANES)
                real = first[2 * f * radix : (2 * f + 1) * radix, cols]
                imag = first[(2 * f + 1) * radix : (2 * f + 2) * radix, cols]
                place = pl.ds((side * half + f) * GROUP + index, radix, stride=rows)
                turned_re[place, :] = real * twist_ref[0] - imag * twist_ref[1]
                turned_im[place, :] = real * twist_ref[1] + imag * twist_ref[0]

    def some_stations(pair, carry):
        for step in range(TOGETHER):
            station(TOGETHER * pair + step, 2 * step)
        return carry

    lax.fori_loop(0, GROUP // TOGETHER, some_stations, 0)
    batch = 16
    e2_cos = e2_ref[0].reshape(rows, LANES)
    e2_sin = e2_ref[1].reshape(rows, LANES)
    e1_cos = e1_ref[0].reshape(rows, radix)
    e1_sin = e1_ref[1].reshape(rows, radix)
    for start in range(0, radix, batch):
        block = slice(start * rows, (start + batch) * rows)
        high, low = split_bf16(jnp.concatenate([turned_re[block, :], turned_im[block, :]], axis=1))
        second = dot(high, w2h_ref[...]) + dot(low, w2h_ref[...]) + dot(high, w2l_ref[...])
        for step in range(batch):
            c1 = start + step
            real = second[step * rows : (step + 1) * rows, :LANES]
            imag = second[step * rows : (step + 1) * rows, LANES:]
            one_cos = e1_cos[:, c1 : c1 + 1]
            one_sin = e1_sin[:, c1 : c1 + 1]
            cosine = e2_cos * one_cos - e2_sin * one_sin
            sine = e2_sin * one_cos + e2_cos * one_sin
            cols = slice(c1 * LANES, (c1 + 1) * LANES)
            shape = (frames, GROUP, LANES)
            out_ref[0, :, :, cols] = (real * cosine - imag * sine).reshape(shape).astype(jnp.bfloat16)
            out_ref[1, :, :, cols] = (real * sine + imag * cosine).reshape(shape).astype(jnp.bfloat16)


def reorder_kernel(picked_ref, early_ref, late_ref, out_ref):
    lines, channels = early_ref.shape
    tile = out_ref.shape[2]
    chunk = 512
    totals = [None, None]
    for start in range(0, channels, chunk):
        counter = lax.broadcasted_iota(jnp.int32, (chunk, tile), 0) + start
        hot = jnp.where(counter == picked_ref[0], 1.0, 0.0).astype(jnp.bfloat16)
        for side, ref in enumerate((early_ref, late_ref)):
            term = dot(ref[:, start : start + chunk], hot)
            totals[side] = term if totals[side] is None else totals[side] + term
    out_ref[0, :lines] = totals[0].astype(jnp.bfloat16)
    out_ref[0, lines:] = totals[1].astype(jnp.bfloat16)


def correlate_kernel(data_ref, out_ref, data, acc):
    segs, halves, parts, frames, stations, tile = data_ref.shape
    count = segs * halves * frames
    part_count = segs * frames
    for part in range(2):
        for side in range(halves):
            block = data_ref[:, side, part].reshape(part_count, stations, tile)
            data[part, side * part_count : (side + 1) * part_count] = block.astype(jnp.float32)
    scale = 1.0 / count

    for tile_a in range(stations // SUB):
        low = tile_a * SUB
        width = stations - low

        def one_row(pair, carry):
            mine = [low + ROWS * pair + i for i in range(ROWS)]

            def frame_step(f, sums):
                b_re = data[0, f, low:, :]
                b_im = data[1, f, low:, :]
                result = []
                for slot, a in enumerate(mine):
                    a_re = data[0, f, pl.ds(a, 1), :]
                    a_im = data[1, f, pl.ds(a, 1), :]
                    result.append(sums[2 * slot] + (a_re * b_re + a_im * b_im))
                    result.append(sums[2 * slot + 1] + (a_im * b_re - a_re * b_im))
                return tuple(result)

            zero = jnp.zeros((width, tile), jnp.float32)
            sums = lax.fori_loop(0, count, frame_step, (zero,) * (2 * ROWS), unroll=4)
            for slot, a in enumerate(mine):
                place = pl.ds(pl.multiple_of(a * stations + low, 8), width)
                acc[0, place, :] = sums[2 * slot] * scale
                acc[1, place, :] = sums[2 * slot + 1] * scale
            return carry

        lax.fori_loop(0, SUB // ROWS, one_row, 0)
    diagonal = acc[0, pl.ds(0, stations, stride=stations + 1), :]
    line = lax.broadcasted_iota(jnp.int32, (SUB, tile), 0)
    for a in range(stations):
        own = a // SUB * SUB
        for low in range(0, own, SUB):
            spot = a * stations + low
            acc[0, spot : spot + SUB, :] = -acc[1, pl.ds(low * stations + a, SUB, stride=stations), :]
        spot = slice(a * stations + own, a * stations + own + SUB)
        acc[0, spot, :] = jnp.where(line + own >= a, acc[0, spot, :], acc[1, spot, :])
    pairs = stations * stations
    out_ref[0, :pairs, :] = acc[0].astype(jnp.bfloat16)
    out_ref[0, pairs:, :] = split_bf16(diagonal)[1]


def spread_kernel(own_ref, packed_ref, out_ref, packed, acc):
    tile = packed_ref.shape[2]
    pairs = acc.shape[1]
    stations = packed_ref.shape[1] - pairs
    packed[...] = packed_ref[0].astype(jnp.float32)
    line = lax.broadcasted_iota(jnp.int32, (SUB, tile), 0)
    for a in range(stations):
        for low in range(0, stations, SUB):
            spot = slice(a * stations + low, a * stations + low + SUB)
            direct = packed[spot, :]
            mirror = packed[pl.ds(low * stations + a, SUB, stride=stations), :]
            if low > a:
                real, imag = direct, -mirror
            elif low + SUB <= a:
                real, imag = mirror, direct
            else:
                fix = packed[pairs + a : pairs + a + 1, :]
                b = line + low
                real = jnp.where(b >= a, direct, mirror) + jnp.where(b == a, fix, 0.0)
                imag = jnp.where(b < a, direct, jnp.where(b == a, 0.0, -mirror))
            acc[0, spot, :] = real
            acc[1, spot, :] = imag
    for part in range(2):
        for start in range(0, pairs, LANES):
            out_ref[part, 0, :, start : start + LANES] = acc[part, start : start + LANES, :].T


def shards(samples, delay_knots, sample_delays, owner_map, filter_taps):
    channels = filter_taps.shape[1]
    stations = samples.shape[1]
    seg_len = samples.shape[2]
    frames = seg_len // channels
    devices = lax.axis_size("row")
    position = lax.axis_index("row")
    radix = channels // LANES
    items = channels // devices
    tail_len = TAPS * channels
    route = [(i, i + 1) for i in range(devices - 1)]
    tail, prev_knots = lax.ppermute((samples[:, :, seg_len - tail_len :], delay_knots), "row", route)
    delays = jnp.stack(
        [
            lax.dynamic_index_in_dim(sample_delays, position, 1, keepdims=False),
            lax.dynamic_index_in_dim(sample_delays, jnp.maximum(position - 1, 0), 1, keepdims=False),
        ]
    )
    knots_own = delay_knots[:, :, 0].astype(jnp.float32)
    knots_prev = jnp.where(position == 0, knots_own, prev_knots[:, :, 0].astype(jnp.float32))
    weights = ((jnp.arange(frames, dtype=jnp.float32) + 1.0) / frames)[:, None]
    track = (1.0 - weights) * knots_prev[:, None] + weights * knots_own[:, None]
    turn = 2.0 * math.pi * track[0][..., None]
    coarse = (jnp.arange(LANES, dtype=jnp.float32) * radix - channels / 2) / channels
    fine = jnp.arange(radix, dtype=jnp.float32) / channels
    angle_two = turn * coarse + track[1][..., None]
    angle_one = turn * fine
    e2 = jnp.stack([jnp.cos(angle_two), jnp.sin(angle_two)])
    e1 = jnp.stack([jnp.cos(angle_one), jnp.sin(angle_one)])

    w_real, w_imag = block_matrix(radix, 1.0)
    section_one = np.block([[w_real, -w_imag], [w_imag, w_real]])
    section_one = np.kron(np.eye(frames // 4), section_one).astype(np.float32)
    w_real, w_imag = block_matrix(LANES, 1.0 / math.sqrt(channels))
    section_two = np.block([[w_real, w_imag], [-w_imag, w_real]]).astype(np.float32)
    w1h = section_one.astype(jnp.bfloat16)
    w1l = (section_one - w1h.astype(np.float32)).astype(jnp.bfloat16)
    w2h = section_two.astype(jnp.bfloat16)
    w2l = (section_two - w2h.astype(np.float32)).astype(jnp.bfloat16)
    twist = 2.0 * math.pi / channels * (np.arange(radix)[:, None] * np.arange(LANES)[None, :])
    twist = np.stack([np.cos(twist), -np.sin(twist)]).astype(np.float32)

    part_frames = frames // 2
    rows = part_frames * GROUP
    part_rows = part_frames * radix
    whole = lambda *shape: pl.BlockSpec(shape, lambda g: (0,) * len(shape))
    blocks = samples.reshape(2, stations, frames * radix, LANES)
    taps = filter_taps.reshape(TAPS, radix, LANES)

    def spectra(side, history, which):
        return pl.pallas_call(
            partial(spectra_kernel, which),
            grid=(stations // GROUP,),
            in_specs=[
                pl.BlockSpec(memory_space=pltpu.SMEM),
                pl.BlockSpec((2, GROUP, part_rows, LANES), lambda g: (0, g, side, 0)),
                pl.BlockSpec((2, GROUP, TAPS * radix, LANES), lambda g: (0, g, 0, 0)),
                whole(TAPS, radix, LANES),
                whole(*w1h.shape),
                whole(*w1l.shape),
                whole(2, radix, LANES),
                whole(*w2h.shape),
                whole(*w2l.shape),
                pl.BlockSpec((2, part_frames, GROUP, radix), lambda g: (0, side, g, 0)),
                pl.BlockSpec((2, part_frames, GROUP, LANES), lambda g: (0, side, g, 0)),
            ],
            out_specs=pl.BlockSpec((2, part_frames, GROUP, channels), lambda g: (0, 0, g, 0)),
            out_shape=jax.ShapeDtypeStruct((2, part_frames, stations, channels), jnp.bfloat16),
            scratch_shapes=[
                pltpu.VMEM((2 * TOGETHER, (part_frames + TAPS) * radix + 8, LANES), jnp.float32),
                pltpu.VMEM((2 * TOGETHER, (part_frames + TAPS - 1) * radix, LANES), jnp.float32),
                pltpu.VMEM((radix * rows, LANES), jnp.float32),
                pltpu.VMEM((radix * rows, LANES), jnp.float32),
            ],
            compiler_params=pltpu.CompilerParams(vmem_limit_bytes=40 * 2**20),
            cost_estimate=pl.CostEstimate(
                flops=8 * 10**9, bytes_accessed=8 * 2**20, transcendentals=0
            ),
        )(delays, blocks, history, taps, w1h, w1l, twist, w2h, w2l, e1, e2)

    lines = frames * stations
    late = spectra(1, blocks, 0).reshape(lines, channels)
    early = spectra(0, tail.reshape(2, stations, TAPS * radix, LANES), 1).reshape(lines, channels)

    members = DUMP_SEGS
    dump_count = devices // members
    share = items * dump_count
    picked = (owner_map % radix * LANES + owner_map // radix).reshape(dump_count, members, items)
    mine = position // members
    picked = jnp.roll(picked, -mine, axis=0)
    picked = picked.transpose(1, 0, 2).reshape(members, 1, share)
    packed = pl.pallas_call(
        reorder_kernel,
        grid=(members,),
        in_specs=[
            pl.BlockSpec((1, 1, share), lambda d: (d, 0, 0)),
            pl.BlockSpec((lines, channels), lambda d: (0, 0)),
            pl.BlockSpec((lines, channels), lambda d: (0, 0)),
        ],
        out_specs=pl.BlockSpec((1, 2 * lines, share), lambda d: (d, 0, 0)),
        out_shape=jax.ShapeDtypeStruct((members, 2 * lines, share), jnp.bfloat16),
        compiler_params=pltpu.CompilerParams(vmem_limit_bytes=50 * 2**20),
    )(picked, early, late)

    near = [[g * members + i for i in range(members)] for g in range(dump_count)]
    received = lax.all_to_all(
        packed, "row", split_axis=0, concat_axis=0, tiled=True, axis_index_groups=near
    )
    received = received.reshape(members, 2, 2, part_frames, stations, share)
    pairs = stations * stations
    height = pairs + stations
    direct = items % LANES == 0
    width = items if direct else share
    per = width // LANES

    def correlate(first):
        return pl.pallas_call(
            correlate_kernel,
            grid=(per,),
            in_specs=[
                pl.BlockSpec(
                    (members, 2, 2, part_frames, stations, LANES),
                    lambda m: (0, 0, 0, 0, 0, first + m),
                ),
            ],
            out_specs=pl.BlockSpec((1, height, LANES), lambda m: (0, 0, m)),
            out_shape=jax.ShapeDtypeStruct((1, height, width), jnp.bfloat16),
            scratch_shapes=[
                pltpu.VMEM((2, members * frames, stations, LANES), jnp.float32),
                pltpu.VMEM((2, pairs, LANES), jnp.float32),
            ],
            compiler_params=pltpu.CompilerParams(vmem_limit_bytes=40 * 2**20),
            cost_estimate=pl.CostEstimate(
                flops=8 * 10**9, bytes_accessed=8 * 2**20, transcendentals=0
            ),
        )(received)

    if not direct:
        everything = correlate(0)
    gathered = [None] * dump_count
    for k in list(range(1, dump_count)) + [0]:
        if direct:
            product = correlate(k * per)
        else:
            product = everything[:, :, k * items : (k + 1) * items]
        if k:
            route = [(i, (i + k * members) % devices) for i in range(devices)]
            product = lax.ppermute(product, "row", route)
        gathered[k] = product
    gathered = jnp.concatenate(gathered, axis=0)
    tile = LANES if direct else items
    return pl.pallas_call(
        spread_kernel,
        grid_spec=pltpu.PrefetchScalarGridSpec(
            num_scalar_prefetch=1,
            grid=(dump_count, items // tile),
            in_specs=[pl.BlockSpec((1, height, tile), lambda k, m, own: (k, 0, m))],
            out_specs=pl.BlockSpec(
                (2, 1, tile, pairs),
                lambda k, m, own: (0, lax.rem(own[0] + dump_count - k, dump_count), m, 0),
            ),
            scratch_shapes=[
                pltpu.VMEM((height, tile), jnp.float32),
                pltpu.VMEM((2, pairs, tile), jnp.float32),
            ],
        ),
        out_shape=jax.ShapeDtypeStruct((2, dump_count, items, pairs), jnp.float32),
        compiler_params=pltpu.CompilerParams(vmem_limit_bytes=40 * 2**20),
    )(jnp.full((1,), mine, jnp.int32), gathered)


def solution(mesh):
    placed = (P(None, "groups", "row"), P(None, "groups", "row"), P("groups", None), P(), P())
    return jax.shard_map(
        shards,
        mesh=mesh,
        in_specs=placed,
        out_specs=P(None, "groups", "row", None),
        check_vma=False,
    )
```
